32 devices in a mesh: dp: 8 (over z, y), section: 2 (over x), mp: 2 (over core).
Axes of the slice: x: 2, y: 2, z: 4, core: 2. Of those that a mesh axis runs over, the one named last changes fastest.
Arguments:
- enc_input: bfloat16 [8, 2, 64, 4096], P('dp', None, 'mp'), may hold values from -6 to 6
- dec_input: bfloat16 [8, 2, 64, 4096], P('dp', None, 'mp'), may hold values from -6 to 6
- enc_lengths: int32 [8, 2, 3], P('dp'), may hold values from 1 to 32, 64 in all within a row
- dec_lengths: int32 [8, 2, 3], P('dp'), may hold values from 1 to 32, 64 in all within a row
- w_query: bfloat16 [2, 4096, 2048], P('section', 'dp', 'mp'), may hold values from -0.09375 to 0.09375
- w_key: bfloat16 [2, 4096, 2048], P('section', 'dp', 'mp'), may hold values from -0.09375 to 0.09375
- w_value: bfloat16 [2, 4096, 2048], P('section', 'dp', 'mp'), may hold values from -0.09375 to 0.09375
- w_output: bfloat16 [2, 2048, 4096], P('section', 'mp', 'dp'), may hold values from -0.125 to 0.125
- layer_gains: float32 [2, 4096], P('section'), may hold values from 0.1 to 1.9
- final_gain: float32 [4096], replicated, may hold values from 0.1 to 1.9
- cotangent: bfloat16 [8, 2, 64, 4096], P('dp', None, 'mp'), may hold values from -6 to 6
Outputs:
- layer_outputs: bfloat16 [2, 8, 2, 64, 4096], P('section', 'dp', None, 'mp')
- input_grads: bfloat16 [2, 8, 2, 64, 4096], P('section', 'dp', None, 'mp')
- gain_grads: float32 [2, 4096], P('section')
- final_grad: float32 [4096], replicated
The draws below stay inside these ranges and needn't reach their ends.
Inputs may be any that keep to these rules, and one draw needn't show every extreme that they name: `enc_lengths`: each row of lengths sums to 64; every row's largest length is exactly 32. `dec_lengths`: each row of lengths sums to 64; every row's largest length is exactly 32.
All inputs are finite; a program needn't handle non-finite values.
Results may differ from the reference program's by a relative error of at most 0.019.
Values may be sent and summed in bfloat16 or wider, within the bound.
A program may use at most 128 MiB of HBM per device.

```python
import math
import jax
import jax.numpy as jnp
import numpy as np
from jax import lax

D = 4096
HD = 256
HW = 2048
ROWS = 64
MICRO = 2
SEGS = 3
SECTIONS = 2
ENC_SECTIONS = 1
GROUPS = 8
N_MP = 2


def level_of(rng, dims, pieces, smallest, high):
    loudness = 1.0
    for dim, parts in pieces:
        steps = jax.random.uniform(jax.random.fold_in(jax.random.fold_in(rng, 6), dim), (parts,), jnp.float32, smallest / len(pieces), high / len(pieces))
        loudness = loudness * jnp.repeat(jnp.exp(steps), dims[dim] // parts).reshape((-1,) + (1,) * (len(dims) - 1 - dim))
    return loudness


def split_up(amount, total, limit, lean):
    weights = [(1 << 20) // math.isqrt(standing ** lean) + 1 for standing in range(2, amount + 1)]
    surplus, holding = total - limit - (amount - 1), [1] * (amount - 1)
    while surplus > 0:
        candidates = [i for i in range(amount - 1) if holding[i] < limit]
        mass, left = sum([weights[i] for i in candidates]), surplus
        for i in candidates:
            more = min(limit - holding[i], max(1, left * weights[i] // mass), surplus)
            holding[i] = holding[i] + more
            surplus = surplus - more
    return np.array([limit] + holding)


def ragged(own_key, number_of, total, most, skew):
    if number_of == 2:
        one = jax.random.randint(own_key, (), max(1, total - most), min(most, total - 1) + 1)
        return jnp.stack([one, total - one])
    sizes = jnp.asarray(split_up(number_of, total, most, skew), jnp.int32)
    couples = (number_of - 1) // 2
    source_of, receiver = sizes[1:1 + 2 * couples:2], sizes[2:2 + 2 * couples:2]
    margin = jnp.minimum(source_of - 1, most - receiver)
    passed = jax.random.randint(jax.random.fold_in(own_key, 1), (couples,), 0, 1 << 20) % (margin + 1)
    sizes = sizes.at[1:1 + 2 * couples:2].set(source_of - passed).at[2:2 + 2 * couples:2].set(receiver + passed)
    return sizes[jax.random.permutation(jax.random.fold_in(own_key, 2), number_of)]


def scatter_about(key, extent, scale, bound, shards=(), held_as=jnp.bfloat16):
    entries = jax.random.normal(key, extent, jnp.float32) * scale
    if len(shards) > 0:
        entries = level_of(key, extent, shards, -0.22, 0.18) * entries
    return jnp.clip(entries, min=-bound, max=bound).astype(held_as)


def setup_inputs(seed: int = 0) -> dict:
    splits = jax.random.split(jax.random.key(seed), 12)
    return {
        "enc_input": scatter_about(splits[0], (GROUPS, MICRO, ROWS, D), 1.0, 6.0, ((0, 8), (2, 2))),
        "dec_input": scatter_about(splits[1], (GROUPS, MICRO, ROWS, D), 1.0, 6.0, ((0, 8), (2, 2))),
        "enc_lengths": jax.vmap(lambda own: ragged(own, SEGS, ROWS, ROWS // 2, 2))(jax.random.split(splits[2], GROUPS * MICRO)).reshape((GROUPS, MICRO, SEGS)).astype(jnp.int32),
        "dec_lengths": jax.vmap(lambda own: ragged(own, SEGS, ROWS, ROWS // 2, 2))(jax.random.split(splits[3], GROUPS * MICRO)).reshape((GROUPS, MICRO, SEGS)).astype(jnp.int32),
        "w_query": scatter_about(splits[4], (SECTIONS, D, HW), D ** -0.5, 0.09375, ((0, 2), (1, 8), (2, 2))),
        "w_key": scatter_about(splits[5], (SECTIONS, D, HW), D ** -0.5, 0.09375, ((0, 2), (1, 8), (2, 2))),
        "w_value": scatter_about(splits[6], (SECTIONS, D, HW), D ** -0.5, 0.09375, ((0, 2), (1, 8), (2, 2))),
        "w_output": scatter_about(splits[7], (SECTIONS, HW, D), HW ** -0.5, 0.125, ((0, 2), (1, 2), (2, 8))),
        "layer_gains": jnp.clip(1.0 + 0.18 * jax.random.normal(splits[8], (SECTIONS, D), jnp.float32), 0.1, 1.9),
        "final_gain": jnp.clip(1.0 + 0.18 * jax.random.normal(splits[9], (D,), jnp.float32), 0.1, 1.9),
        "cotangent": scatter_about(splits[10], (GROUPS, MICRO, ROWS, D), 1.0, 6.0, ((0, 8), (2, 2))),
    }


epsilon = 1e-06

def rounded(array):
    return lax.optimization_barrier(array.astype(jnp.bfloat16)).astype(jnp.float32)

def segment_ids(lengths, count):
    ends = jnp.cumsum(lengths, axis=-1).astype(jnp.int32)
    position = jnp.arange(count, dtype=jnp.int32)
    above = (position[None, :, None] >= ends[:, None, :-1]).astype(jnp.int32)
    return lax.optimization_barrier(jnp.sum(above, axis=-1)).astype(jnp.int32)

def rms_norm(inputs, norm_gain):
    floats = inputs.astype(jnp.float32)
    spread = jnp.sqrt(lax.optimization_barrier(jnp.mean(floats * floats, axis=-1, keepdims=True)) + epsilon)
    normal = floats / spread
    return (normal * norm_gain, normal, spread)

def norm_back(grad_out, normal, spread, norm_gain):
    scaled = grad_out * norm_gain
    return (scaled - normal * lax.optimization_barrier(jnp.mean(scaled * normal, axis=-1, keepdims=True))) / spread

def attend(hidden, source, w_query, w_key, w_value, w_output, seg_query, seg_key, head_size):
    row_count = hidden.shape[0]
    query = rounded(jnp.dot(hidden, w_query, preferred_element_type=jnp.float32))
    key_rows = rounded(jnp.dot(source, w_key, preferred_element_type=jnp.float32))
    value_rows = rounded(jnp.dot(source, w_value, preferred_element_type=jnp.float32))
    query_heads = query.reshape(row_count, -1, head_size)
    key_heads = key_rows.reshape(row_count, -1, head_size)
    value_heads = value_rows.reshape(row_count, -1, head_size)
    scores = jnp.einsum('qhd,khd->hqk', query_heads, key_heads) * head_size ** (-0.5)
    same_doc = seg_query[:, None] == seg_key[None, :]
    scores = jnp.where(same_doc[None], scores, -1e+30)
    row_max = lax.optimization_barrier(jnp.max(scores, axis=-1, keepdims=True))
    exponent = jnp.exp(scores - row_max)
    attention = exponent / lax.optimization_barrier(jnp.sum(exponent, axis=-1, keepdims=True))
    mixed = jnp.einsum('hqk,khd->qhd', rounded(attention), value_heads).reshape(row_count, -1)
    partial_value = jnp.dot(mixed.astype(jnp.bfloat16), w_output, preferred_element_type=jnp.float32)
    return (partial_value, (query, key_rows, value_rows, attention))

def attend_back(grad_in, stored, w_query, w_key, w_value, w_output, head_size):
    query, key_rows, value_rows, attention = stored
    row_count = grad_in.shape[0]
    scale = head_size ** (-0.5)
    grad_mixed = rounded(jnp.dot(grad_in, w_output.T, preferred_element_type=jnp.float32))
    grad_heads = grad_mixed.reshape(row_count, -1, head_size)
    query_heads = query.reshape(row_count, -1, head_size)
    key_heads = key_rows.reshape(row_count, -1, head_size)
    value_heads = value_rows.reshape(row_count, -1, head_size)
    grad_value = rounded(jnp.einsum('hqk,qhd->khd', rounded(attention), grad_heads)).reshape(row_count, -1)
    grad_att = jnp.einsum('qhd,khd->hqk', grad_heads, value_heads)
    grad_scores = attention * (grad_att - lax.optimization_barrier(jnp.sum(attention * grad_att, axis=-1, keepdims=True))) * scale
    grad_query = rounded(jnp.einsum('hqk,khd->qhd', grad_scores, key_heads)).reshape(row_count, -1)
    grad_key = rounded(jnp.einsum('hqk,qhd->khd', grad_scores, query_heads)).reshape(row_count, -1)
    grad_hidden = jnp.dot(grad_query.astype(jnp.bfloat16), w_query.T, preferred_element_type=jnp.float32)
    grad_source = jnp.dot(grad_key.astype(jnp.bfloat16), w_key.T, preferred_element_type=jnp.float32)
    grad_source = grad_source + jnp.dot(grad_value.astype(jnp.bfloat16), w_value.T, preferred_element_type=jnp.float32)
    return (grad_hidden, grad_source)

def reference(enc_input, dec_input, enc_lengths, dec_lengths, w_query, w_key, w_value, w_output, layer_gains, final_gain, cotangent):
    batch = GROUPS * MICRO
    group_width = HW // N_MP
    enc_seg = segment_ids(enc_lengths.reshape(batch, SEGS), ROWS)
    dec_seg = segment_ids(dec_lengths.reshape(batch, SEGS), ROWS)

    def group_params(layer, group):
        lower = group * group_width
        upper = lower + group_width
        return (w_query[layer][:, lower:upper], w_key[layer][:, lower:upper], w_value[layer][:, lower:upper], w_output[layer][lower:upper, :])

    def forward(layer, inputs, source, seg_query):
        hidden = rms_norm(inputs, layer_gains[layer])[0].astype(jnp.bfloat16)
        if layer < ENC_SECTIONS:
            source = hidden
        total = jnp.zeros((batch, ROWS, D), jnp.float32)
        stores = []
        for group in range(N_MP):
            params = group_params(layer, group)
            partial_value, stored = jax.vmap(lambda a, b, c, e: attend(a, b, params[0], params[1], params[2], params[3], c, e, HD))(hidden, source, seg_query, enc_seg)
            total = total + rounded(partial_value)
            stores.append(stored)
        return ((inputs.astype(jnp.float32) + total).astype(jnp.bfloat16), stores)
    outputs = []
    inputs_all = []
    stores_all = []
    current = enc_input.reshape(batch, ROWS, D)
    source = None
    for layer in range(SECTIONS):
        if layer == ENC_SECTIONS:
            encoded_norm, enc_normal, enc_spread = rms_norm(current, final_gain)
            source = encoded_norm.astype(jnp.bfloat16)
            current = dec_input.reshape(batch, ROWS, D)
        seg_query = enc_seg if layer < ENC_SECTIONS else dec_seg
        inputs_all.append(current)
        current, stores = forward(layer, current, source, seg_query)
        stores_all.append(stores)
        outputs.append(current)
    grad = cotangent.reshape(batch, ROWS, D)
    grads = [None] * SECTIONS
    gain_list = [None] * SECTIONS
    grad_encoded = jnp.zeros((batch, ROWS, D), jnp.float32)
    final_grad = jnp.zeros((D,), jnp.float32)
    for layer in reversed(range(SECTIONS)):
        if layer == ENC_SECTIONS - 1:
            grad = norm_back(grad_encoded, enc_normal, enc_spread, final_gain).astype(jnp.bfloat16)
            final_grad = lax.optimization_barrier(jnp.sum(grad_encoded * enc_normal, axis=(0, 1)))
        normal, spread = rms_norm(inputs_all[layer], layer_gains[layer])[1:]
        total = jnp.zeros((batch, ROWS, D), jnp.float32)
        gain_total = jnp.zeros((D,), jnp.float32)
        for group in range(N_MP):
            params = group_params(layer, group)
            grad_hidden, grad_source = jax.vmap(lambda a, b: attend_back(a, b, params[0], params[1], params[2], params[3], HD))(grad, stores_all[layer][group])
            if layer < ENC_SECTIONS:
                grad_hidden = grad_hidden + grad_source
            else:
                grad_encoded = grad_encoded + grad_source
            total = total + rounded(norm_back(grad_hidden, normal, spread, layer_gains[layer]))
            gain_total = gain_total + lax.optimization_barrier(jnp.sum(grad_hidden * normal, axis=(0, 1)))
        grad = (grad.astype(jnp.float32) + total).astype(jnp.bfloat16)
        grads[layer] = grad
        gain_list[layer] = gain_total
    layer_outputs = jnp.stack(outputs).reshape(SECTIONS, GROUPS, MICRO, ROWS, D)
    input_grads = jnp.stack(grads).reshape(SECTIONS, GROUPS, MICRO, ROWS, D)
    return (layer_outputs, input_grads, jnp.stack(gain_list), final_grad)
```

```python
import jax
import jax.numpy as jnp
from jax import lax
from jax.sharding import PartitionSpec as P

HD = 256

epsilon = 1e-06


def gather_weights(wq, wk, wv, wo):
    return (
        lax.all_gather(wq, "dp", axis=0, tiled=True),
        lax.all_gather(wk, "dp", axis=0, tiled=True),
        lax.all_gather(wv, "dp", axis=0, tiled=True),
        lax.all_gather(wo, "dp", axis=1, tiled=True),
    )


def segment_ids(lengths, count):
    ends = jnp.cumsum(lengths, axis=-1)
    position = jnp.arange(count, dtype=jnp.int32)
    above = (position[None, :, None] >= ends[:, None, :-1]).astype(jnp.int32)
    return jnp.sum(above, axis=-1)


def rms_norm(inputs, norm_gain):
    floats = inputs.astype(jnp.float32)
    spread = jnp.sqrt(jnp.mean(floats * floats, axis=-1, keepdims=True) + epsilon)
    normal = floats / spread
    return (normal * norm_gain, normal, spread)


def norm_back(grad_out, normal, spread, norm_gain):
    scaled = grad_out * norm_gain
    return (scaled - normal * jnp.mean(scaled * normal, axis=-1, keepdims=True)) / spread


def dot(left, right):
    return jnp.dot(left, right, preferred_element_type=jnp.float32)


def dot_t(left, right):
    return lax.dot_general(left, right, (((1,), (1,)), ((), ())), preferred_element_type=jnp.float32)


def heads_of(rows, micro):
    return rows.reshape(micro, rows.shape[0] // micro, -1, HD)


def heads_einsum(spec, left, right):
    return jnp.einsum(spec, left, right, preferred_element_type=jnp.float32)


def softmax_scores(query, key, same_doc):
    scores = heads_einsum("mqhd,mkhd->mhqk", query, key) * HD ** (-0.5)
    scores = jnp.where(same_doc[:, None], scores, -1e30)
    exponent = jnp.exp(scores - jnp.max(scores, axis=-1, keepdims=True))
    return exponent / jnp.sum(exponent, axis=-1, keepdims=True)


def partner(array, axis):
    return lax.ppermute(array, axis, [(0, 1), (1, 0)])


def sum_of_all(array):
    array = array + partner(array, "mp")
    count = lax.axis_size("dp")
    step = 1
    while step < count:
        array = array + lax.ppermute(array, "dp", [(i, i ^ step) for i in range(count)])
        step *= 2
    return array


def shards(
    enc_input, dec_input, enc_lengths, dec_lengths, w_query, w_key, w_value, w_output,
    layer_gains, final_gain, cotangent,
):
    is_encoder = lax.axis_index("section") == 0
    core = lax.axis_index("mp")
    micro, piece, width = enc_input.shape[1:]
    count = piece * lax.axis_size("mp")
    rows = micro * count
    gain = layer_gains[0]

    def all_rows(pieces):
        return lax.all_gather(pieces, "mp", axis=1, tiled=True).reshape(rows, width)

    def add_pieces(partial_rows):
        halves = partial_rows.astype(jnp.bfloat16).reshape(micro, 2, piece, width)
        mine = lax.dynamic_index_in_dim(halves, core, 1, keepdims=False)
        other = lax.dynamic_index_in_dim(halves, 1 - core, 1, keepdims=False)
        return mine.astype(jnp.float32) + partner(other, "mp").astype(jnp.float32)

    enc_seg = segment_ids(enc_lengths[0], count)
    dec_seg = segment_ids(dec_lengths[0], count)
    query_seg = jnp.where(is_encoder, enc_seg, dec_seg)
    same_doc = query_seg[:, :, None] == enc_seg[:, None, :]
    entry = jnp.where(is_encoder, enc_input[0], dec_input[0])
    inputs = all_rows(entry)
    grad_last = all_rows(cotangent[0])
    full_q, full_k, full_v, full_o = gather_weights(
        w_query[0], w_key[0], w_value[0], w_output[0]
    )
    hidden_f, normal, spread = rms_norm(inputs, gain)
    hidden = hidden_f.astype(jnp.bfloat16)
    query = heads_of(dot(hidden, full_q).astype(jnp.bfloat16), micro)

    def forward(source):
        key = heads_of(dot(source, full_k).astype(jnp.bfloat16), micro)
        value = heads_of(dot(source, full_v).astype(jnp.bfloat16), micro)
        attention = softmax_scores(query, key, same_doc)
        mixed = heads_einsum("mhqk,mkhd->mqhd", attention.astype(jnp.bfloat16), value)
        part = dot(mixed.astype(jnp.bfloat16).reshape(rows, -1), full_o)
        result = (entry.astype(jnp.float32) + add_pieces(part)).astype(jnp.bfloat16)
        return result, key, value, attention

    enc_out = forward(hidden)[0]
    from_enc = lax.ppermute(enc_out, "section", [(0, 1)])
    encoded = jnp.where(is_encoder, enc_out, from_enc)
    normed, enc_normal, enc_spread = rms_norm(encoded, final_gain)
    source = jnp.where(is_encoder, hidden, all_rows(normed.astype(jnp.bfloat16)))
    layer_out, key, value, attention = forward(source)
    attention_b = attention.astype(jnp.bfloat16)

    def score_grads(grad_rows):
        grad_mixed = heads_of(dot_t(grad_rows, full_o).astype(jnp.bfloat16), micro)
        grad_value = heads_einsum("mhqk,mqhd->mkhd", attention_b, grad_mixed)
        grad_att = heads_einsum("mqhd,mkhd->mhqk", grad_mixed, value)
        shared = jnp.sum(attention * grad_att, axis=-1, keepdims=True)
        grad_scores = (attention * (grad_att - shared) * HD ** (-0.5)).astype(jnp.bfloat16)
        grad_key = heads_einsum("mhqk,mqhd->mkhd", grad_scores, query)
        grad_source = dot_t(grad_key.astype(jnp.bfloat16).reshape(rows, -1), full_k)
        grad_source = grad_source + dot_t(
            grad_value.astype(jnp.bfloat16).reshape(rows, -1), full_v
        )
        return grad_scores, grad_source

    cross = add_pieces(score_grads(grad_last)[1])
    cross_sent = lax.ppermute(cross.astype(jnp.bfloat16), "section", [(1, 0)])
    cross = jnp.where(is_encoder, cross_sent, cross.astype(jnp.bfloat16)).astype(jnp.float32)
    enc_grads = norm_back(cross, enc_normal, enc_spread, final_gain).astype(jnp.bfloat16)
    final_part = jnp.sum(cross * enc_normal, axis=(0, 1))

    grad_piece = jnp.where(is_encoder, enc_grads, cotangent[0])
    grad_rows = all_rows(grad_piece)
    grad_scores, grad_source = score_grads(grad_rows)
    grad_query = heads_einsum("mhqk,mkhd->mqhd", grad_scores, key)
    grad_hidden = dot_t(grad_query.astype(jnp.bfloat16).reshape(rows, -1), full_q)
    grad_hidden = grad_hidden + jnp.where(is_encoder, grad_source, 0.0)
    grad_part = norm_back(grad_hidden, normal, spread, gain)
    gain_part = jnp.sum(grad_hidden * normal, axis=0)
    totals = sum_of_all(jnp.stack([gain_part, final_part]))
    input_grad = (grad_piece.astype(jnp.float32) + add_pieces(grad_part)).astype(jnp.bfloat16)
    return (layer_out[None, None], input_grad[None, None], totals[:1], totals[1])


def solution(mesh):
    return jax.shard_map(
        shards,
        mesh=mesh,
        in_specs=(
            P("dp", None, "mp", None),
            P("dp", None, "mp", None),
            P("dp", None, None),
            P("dp", None, None),
            P("section", "dp", "mp"),
            P("section", "dp", "mp"),
            P("section", "dp", "mp"),
            P("section", "mp", "dp"),
            P("section", None),
            P(),
            P("dp", None, "mp", None),
        ),
        out_specs=(
            P("section", "dp", None, "mp", None),
            P("section", "dp", None, "mp", None),
            P("section", None),
            P(),
        ),
        check_vma=False,
    )
```

```python
import functools

import jax
import jax.numpy as jnp
from jax import lax
from jax.experimental import pallas as pl
from jax.experimental.pallas import tpu as pltpu
from jax.sharding import PartitionSpec as P

HD = 256
MESH = pl.DeviceIdType.MESH

epsilon = 1e-06


def gather_kernel(
    lines, parts, crossed, wq, wk, wv, wo, oq, ok, ov, oo,
    send_right, send_left, recv_z, send_y, recv_y, local_sem,
):
    me = lax.axis_index("dp")
    a = me // 2
    b = me % 2
    ins = (wq, wk, wv, wo)
    outs = (oq, ok, ov, oo)

    def own(w, p):
        size = ins[w].shape[0] // parts
        return ins[w].at[pl.ds(pl.multiple_of(p * size, size), size), :]

    def slot(w, line, side, p):
        size = ins[w].shape[0] // parts
        block = line * 2 + side
        if w < 3:
            start = block * ins[w].shape[0] + p * size
            return outs[w].at[pl.ds(pl.multiple_of(start, size), size), :]
        cols = ins[w].shape[1]
        return outs[w].at[
            pl.ds(pl.multiple_of(p * size, size), size),
            pl.ds(pl.multiple_of(block * cols, cols), cols),
        ]

    def along(w, p, line, side, right, src=None):
        dst = slot(w, line, side, p)
        sem = (send_right if right else send_left).at[side, w * parts + p, line]
        target = (a + 1) if right else (a - 1)
        return pltpu.make_async_remote_copy(
            src_ref=dst if src is None else src, dst_ref=dst, send_sem=sem,
            recv_sem=recv_z.at[side, w * parts + p, line],
            device_id={"dp": target * 2 + b}, device_id_type=MESH,
        )

    def across(w, p, line, side, src=None):
        dst = slot(w, line, side, p)
        return pltpu.make_async_remote_copy(
            src_ref=dst if src is None else src, dst_ref=dst,
            send_sem=send_y.at[w * parts + p, line],
            recv_sem=recv_y.at[w * parts + p, line],
            device_id={"dp": a * 2 + 1 - b}, device_id_type=MESH,
        )

    def each(first, last, w, body):
        if last[w] > first[w]:
            lax.fori_loop(first[w], last[w], lambda p, c: (body(p), c)[1], 0)

    none = [0] * 4
    split = [parts - crossed[w] for w in range(4)]
    full = [parts] * 4
    has_right = a + 1 < lines
    has_left = a > 0

    barrier = pltpu.get_barrier_semaphore()
    pl.semaphore_signal(barrier, inc=1, device_id={"dp": a * 2 + 1 - b}, device_id_type=MESH)

    @pl.when(has_right)
    def _():
        pl.semaphore_signal(barrier, inc=1, device_id={"dp": me + 2}, device_id_type=MESH)

    @pl.when(has_left)
    def _():
        pl.semaphore_signal(barrier, inc=1, device_id={"dp": me - 2}, device_id_type=MESH)

    peers = 1 + has_right.astype(jnp.int32) + has_left.astype(jnp.int32)
    pl.semaphore_wait(barrier, peers)

    def both_ways(w, p, line, side, src, op):
        @pl.when(has_right)
        def _():
            op(along(w, p, line, side, True, src))

        @pl.when(has_left)
        def _():
            op(along(w, p, line, side, False, src))

    def start(copy):
        copy.start()

    def sent(copy):
        copy.wait_send()

    def begin(w, p):
        across(w, p, a, b, own(w, p)).start()
        both_ways(w, p, a, b, own(w, p), start)

    for w in range(4):
        each(split, full, w, functools.partial(begin, w))
    for w in range(4):
        each(none, split, w, functools.partial(begin, w))
    for w in range(4):
        each(none, full, w, lambda p, w=w: pltpu.make_async_copy(
            own(w, p), slot(w, a, b, p), local_sem.at[w * parts + p]).start())

    def turn(w, p):
        across(w, p, a, 1 - b).wait_recv()
        both_ways(w, p, a, 1 - b, None, start)

    for w in range(4):
        each(split, full, w, functools.partial(turn, w))

    def relay(w, p, dist, side, cross, op):
        @pl.when(a - dist >= 0)
        def _():
            line = a - dist
            if op is start:
                along(w, p, line, side, True).wait_recv()

            @pl.when(has_right)
            def _():
                op(along(w, p, line, side, True))

            if cross:
                op(across(w, p, line, side))

        @pl.when(a + dist < lines)
        def _():
            line = a + dist
            if op is start:
                along(w, p, line, side, False).wait_recv()

            @pl.when(has_left)
            def _():
                op(along(w, p, line, side, False))

            if cross:
                op(across(w, p, line, side))

    def hop(dist, op):
        for w in range(4):
            def crossed_part(p, w=w):
                relay(w, p, dist, b, False, op)
                relay(w, p, dist, 1 - b, False, op)

            each(split, full, w, crossed_part)
            each(none, split, w, lambda p, w=w: relay(w, p, dist, b, True, op))

    def hop_start(dist, c):
        hop(dist, start)
        return c

    def hop_sent(dist, c):
        hop(dist, sent)
        return c

    lax.fori_loop(1, lines, hop_start, 0)
    for w in range(4):
        def arrived(p, w=w):
            def one(line, c):
                across(w, p, line, 1 - b).wait_recv()
                return c

            lax.fori_loop(0, lines, one, 0)

        each(none, split, w, arrived)

    for w in range(4):
        def finish(p, w=w):
            across(w, p, a, b, own(w, p)).wait_send()
            both_ways(w, p, a, b, own(w, p), sent)
            pltpu.make_async_copy(
                own(w, p), slot(w, a, b, p), local_sem.at[w * parts + p]).wait()

        each(none, full, w, finish)
        each(split, full, w, lambda p, w=w: both_ways(w, p, a, 1 - b, None, sent))
    lax.fori_loop(1, lines, hop_sent, 0)


def gather_weights(wq, wk, wv, wo):
    count = lax.axis_size("dp")
    lines = count // 2
    parts = max(1, 16 // lines)
    crossed = (1, 1, 1, 0) if parts > 1 else (0, 0, 0, 0)
    units = 4 * parts
    rows, width = wq.shape
    tall = jax.ShapeDtypeStruct((rows * count, width), wq.dtype)
    wide = jax.ShapeDtypeStruct((wo.shape[0], wo.shape[1] * count), wo.dtype)
    dma = pltpu.SemaphoreType.DMA
    return pl.pallas_call(
        functools.partial(gather_kernel, lines, parts, crossed),
        out_shape=(tall, tall, tall, wide),
        in_specs=[pl.BlockSpec(memory_space=pl.ANY)] * 4,
        out_specs=[pl.BlockSpec(memory_space=pl.ANY)] * 4,
        scratch_shapes=[
            dma((2, units, lines)), dma((2, units, lines)), dma((2, units, lines)),
            dma((units, lines)), dma((units, lines)), dma((units,)),
        ],
        compiler_params=pltpu.CompilerParams(collective_id=0, has_side_effects=True),
    )(wq, wk, wv, wo)


def segment_ids(lengths, count):
    ends = jnp.cumsum(lengths, axis=-1)
    position = jnp.arange(count, dtype=jnp.int32)
    above = (position[None, :, None] >= ends[:, None, :-1]).astype(jnp.int32)
    return jnp.sum(above, axis=-1)


def rms_norm(inputs, norm_gain):
    floats = inputs.astype(jnp.float32)
    spread = jnp.sqrt(jnp.mean(floats * floats, axis=-1, keepdims=True) + epsilon)
    normal = floats / spread
    return (normal * norm_gain, normal, spread)


def norm_back(grad_out, normal, spread, norm_gain):
    scaled = grad_out * norm_gain
    return (scaled - normal * jnp.mean(scaled * normal, axis=-1, keepdims=True)) / spread


def dot(left, right):
    return jnp.dot(left, right, preferred_element_type=jnp.float32)


def dot_t(left, right):
    return lax.dot_general(left, right, (((1,), (1,)), ((), ())), preferred_element_type=jnp.float32)


def heads_of(rows, micro):
    return rows.reshape(micro, rows.shape[0] // micro, -1, HD)


def heads_einsum(spec, left, right):
    return jnp.einsum(spec, left, right, preferred_element_type=jnp.float32)


def softmax_scores(query, key, same_doc):
    scores = heads_einsum("mqhd,mkhd->mhqk", query, key) * HD ** (-0.5)
    scores = jnp.where(same_doc[:, None], scores, -1e30)
    exponent = jnp.exp(scores - jnp.max(scores, axis=-1, keepdims=True))
    return exponent / jnp.sum(exponent, axis=-1, keepdims=True)


def partner(array, axis):
    return lax.ppermute(array, axis, [(0, 1), (1, 0)])


def sum_of_all(array):
    array = array + partner(array, "mp")
    count = lax.axis_size("dp")
    step = 1
    while step < count:
        array = array + lax.ppermute(array, "dp", [(i, i ^ step) for i in range(count)])
        step *= 2
    return array


def shards(
    enc_input, dec_input, enc_lengths, dec_lengths, w_query, w_key, w_value, w_output,
    layer_gains, final_gain, cotangent,
):
    is_encoder = lax.axis_index("section") == 0
    core = lax.axis_index("mp")
    micro, piece, width = enc_input.shape[1:]
    count = piece * lax.axis_size("mp")
    rows = micro * count
    gain = layer_gains[0]

    def all_rows(pieces):
        return lax.all_gather(pieces, "mp", axis=1, tiled=True).reshape(rows, width)

    def add_pieces(partial_rows):
        halves = partial_rows.astype(jnp.bfloat16).reshape(micro, 2, piece, width)
        mine = lax.dynamic_index_in_dim(halves, core, 1, keepdims=False)
        other = lax.dynamic_index_in_dim(halves, 1 - core, 1, keepdims=False)
        return mine.astype(jnp.float32) + partner(other, "mp").astype(jnp.float32)

    enc_seg = segment_ids(enc_lengths[0], count)
    dec_seg = segment_ids(dec_lengths[0], count)
    query_seg = jnp.where(is_encoder, enc_seg, dec_seg)
    same_doc = query_seg[:, :, None] == enc_seg[:, None, :]
    entry = jnp.where(is_encoder, enc_input[0], dec_input[0])
    inputs = all_rows(entry)
    grad_last = all_rows(cotangent[0])
    full_q, full_k, full_v, full_o = gather_weights(
        w_query[0], w_key[0], w_value[0], w_output[0]
    )
    hidden_f, normal, spread = rms_norm(inputs, gain)
    hidden = hidden_f.astype(jnp.bfloat16)
    query = heads_of(dot(hidden, full_q).astype(jnp.bfloat16), micro)

    def forward(source):
        key = heads_of(dot(source, full_k).astype(jnp.bfloat16), micro)
        value = heads_of(dot(source, full_v).astype(jnp.bfloat16), micro)
        attention = softmax_scores(query, key, same_doc)
        mixed = heads_einsum("mhqk,mkhd->mqhd", attention.astype(jnp.bfloat16), value)
        part = dot(mixed.astype(jnp.bfloat16).reshape(rows, -1), full_o)
        result = (entry.astype(jnp.float32) + add_pieces(part)).astype(jnp.bfloat16)
        return result, key, value, attention

    enc_out = forward(hidden)[0]
    from_enc = lax.ppermute(enc_out, "section", [(0, 1)])
    encoded = jnp.where(is_encoder, enc_out, from_enc)
    normed, enc_normal, enc_spread = rms_norm(encoded, final_gain)
    source = jnp.where(is_encoder, hidden, all_rows(normed.astype(jnp.bfloat16)))
    layer_out, key, value, attention = forward(source)
    attention_b = attention.astype(jnp.bfloat16)

    def score_grads(grad_rows):
        grad_mixed = heads_of(dot_t(grad_rows, full_o).astype(jnp.bfloat16), micro)
        grad_value = heads_einsum("mhqk,mqhd->mkhd", attention_b, grad_mixed)
        grad_att = heads_einsum("mqhd,mkhd->mhqk", grad_mixed, value)
        shared = jnp.sum(attention * grad_att, axis=-1, keepdims=True)
        grad_scores = (attention * (grad_att - shared) * HD ** (-0.5)).astype(jnp.bfloat16)
        grad_key = heads_einsum("mhqk,mqhd->mkhd", grad_scores, query)
        grad_source = dot_t(grad_key.astype(jnp.bfloat16).reshape(rows, -1), full_k)
        grad_source = grad_source + dot_t(
            grad_value.astype(jnp.bfloat16).reshape(rows, -1), full_v
        )
        return grad_scores, grad_source

    cross = add_pieces(score_grads(grad_last)[1])
    cross_sent = lax.ppermute(cross.astype(jnp.bfloat16), "section", [(1, 0)])
    cross = jnp.where(is_encoder, cross_sent, cross.astype(jnp.bfloat16)).astype(jnp.float32)
    enc_grads = norm_back(cross, enc_normal, enc_spread, final_gain).astype(jnp.bfloat16)
    final_part = jnp.sum(cross * enc_normal, axis=(0, 1))

    grad_piece = jnp.where(is_encoder, enc_grads, cotangent[0])
    grad_rows = all_rows(grad_piece)
    grad_scores, grad_source = score_grads(grad_rows)
    grad_query = heads_einsum("mhqk,mkhd->mqhd", grad_scores, key)
    grad_hidden = dot_t(grad_query.astype(jnp.bfloat16).reshape(rows, -1), full_q)
    grad_hidden = grad_hidden + jnp.where(is_encoder, grad_source, 0.0)
    grad_part = norm_back(grad_hidden, normal, spread, gain)
    gain_part = jnp.sum(grad_hidden * normal, axis=0)
    totals = sum_of_all(jnp.stack([gain_part, final_part]))
    input_grad = (grad_piece.astype(jnp.float32) + add_pieces(grad_part)).astype(jnp.bfloat16)
    return (layer_out[None, None], input_grad[None, None], totals[:1], totals[1])


def solution(mesh):
    return jax.shard_map(
        shards,
        mesh=mesh,
        in_specs=(
            P("dp", None, "mp", None),
            P("dp", None, "mp", None),
            P("dp", None, None),
            P("dp", None, None),
            P("section", "dp", "mp"),
            P("section", "dp", "mp"),
            P("section", "dp", "mp"),
            P("section", "mp", "dp"),
            P("section", None),
            P(),
            P("dp", None, "mp", None),
        ),
        out_specs=(
            P("section", "dp", None, "mp", None),
            P("section", "dp", None, "mp", None),
            P("section", None),
            P(),
        ),
        check_vma=False,
    )
```

```python
import functools

import jax
import jax.numpy as jnp
from jax import lax
from jax.experimental import pallas as pl
from jax.experimental.pallas import tpu as pltpu
from jax.sharding import PartitionSpec as P

HD = 256
MESH = pl.DeviceIdType.MESH

epsilon = 1e-06


def gather_kernel(
    lines, parts, crossed, wq, wk, wv, wo, oq, ok, ov, oo,
    send_right, send_left, recv_z, send_y, recv_y, local_sem,
):
    me = lax.axis_index("dp")
    a = me // 2
    b = me % 2
    ins = (wq, wk, wv, wo)
    outs = (oq, ok, ov, oo)

    def own(w, p):
        size = ins[w].shape[0] // parts
        return ins[w].at[pl.ds(pl.multiple_of(p * size, size), size), :]

    def slot(w, line, side, p):
        size = ins[w].shape[0] // parts
        block = line * 2 + side
        if w < 3:
            start = block * ins[w].shape[0] + p * size
            return outs[w].at[pl.ds(pl.multiple_of(start, size), size), :]
        cols = ins[w].shape[1]
        return outs[w].at[
            pl.ds(pl.multiple_of(p * size, size), size),
            pl.ds(pl.multiple_of(block * cols, cols), cols),
        ]

    def along(w, p, line, side, right, src=None):
        dst = slot(w, line, side, p)
        sem = (send_right if right else send_left).at[side, w * parts + p, line]
        target = (a + 1) if right else (a - 1)
        return pltpu.make_async_remote_copy(
            src_ref=dst if src is None else src, dst_ref=dst, send_sem=sem,
            recv_sem=recv_z.at[side, w * parts + p, line],
            device_id={"dp": target * 2 + b}, device_id_type=MESH,
        )

    def across(w, p, line, side, src=None):
        dst = slot(w, line, side, p)
        return pltpu.make_async_remote_copy(
            src_ref=dst if src is None else src, dst_ref=dst,
            send_sem=send_y.at[w * parts + p, line],
            recv_sem=recv_y.at[w * parts + p, line],
            device_id={"dp": a * 2 + 1 - b}, device_id_type=MESH,
        )

    def each(first, last, w, body):
        if last[w] > first[w]:
            lax.fori_loop(first[w], last[w], lambda p, c: (body(p), c)[1], 0)

    none = [0] * 4
    split = [parts - crossed[w] for w in range(4)]
    full = [parts] * 4
    has_right = a + 1 < lines
    has_left = a > 0

    barrier = pltpu.get_barrier_semaphore()
    pl.semaphore_signal(barrier, inc=1, device_id={"dp": a * 2 + 1 - b}, device_id_type=MESH)

    @pl.when(has_right)
    def _():
        pl.semaphore_signal(barrier, inc=1, device_id={"dp": me + 2}, device_id_type=MESH)

    @pl.when(has_left)
    def _():
        pl.semaphore_signal(barrier, inc=1, device_id={"dp": me - 2}, device_id_type=MESH)

    peers = 1 + has_right.astype(jnp.int32) + has_left.astype(jnp.int32)
    pl.semaphore_wait(barrier, peers)

    def both_ways(w, p, line, side, src, op):
        @pl.when(has_right)
        def _():
            op(along(w, p, line, side, True, src))

        @pl.when(has_left)
        def _():
            op(along(w, p, line, side, False, src))

    def start(copy):
        copy.start()

    def sent(copy):
        copy.wait_send()

    def begin_across(w, p):
        across(w, p, a, b, own(w, p)).start()

    def begin_along(w, p):
        both_ways(w, p, a, b, own(w, p), start)

    def begin(w, p):
        begin_along(w, p)
        begin_across(w, p)

    for w in range(4):
        each(split, full, w, functools.partial(begin_across, w))
    for w in range(4):
        each(none, split, w, functools.partial(begin, w))
    for w in range(4):
        each(split, full, w, functools.partial(begin_along, w))
    for w in range(4):
        each(none, full, w, lambda p, w=w: pltpu.make_async_copy(
            own(w, p), slot(w, a, b, p), local_sem.at[w * parts + p]).start())

    def turn(w, p):
        across(w, p, a, 1 - b).wait_recv()
        both_ways(w, p, a, 1 - b, None, start)

    for w in range(4):
        each(split, full, w, functools.partial(turn, w))

    def relay(w, p, dist, side, cross, op):
        @pl.when(a - dist >= 0)
        def _():
            line = a - dist
            if op is start:
                along(w, p, line, side, True).wait_recv()

            @pl.when(has_right)
            def _():
                op(along(w, p, line, side, True))

            if cross:
                op(across(w, p, line, side))

        @pl.when(a + dist < lines)
        def _():
            line = a + dist
            if op is start:
                along(w, p, line, side, False).wait_recv()

            @pl.when(has_left)
            def _():
                op(along(w, p, line, side, False))

            if cross:
                op(across(w, p, line, side))

    def hop(dist, op):
        for w in range(4):
            each(none, split, w, lambda p, w=w: relay(w, p, dist, b, True, op))
        for w in range(4):
            def crossed_part(p, w=w):
                relay(w, p, dist, b, False, op)
                relay(w, p, dist, 1 - b, False, op)

            each(split, full, w, crossed_part)

    def hop_start(dist, c):
        hop(dist, start)
        return c

    def hop_sent(dist, c):
        hop(dist, sent)
        return c

    lax.fori_loop(1, lines, hop_start, 0)
    for w in range(4):
        def arrived(p, w=w):
            def one(line, c):
                across(w, p, line, 1 - b).wait_recv()
                return c

            lax.fori_loop(0, lines, one, 0)

        each(none, split, w, arrived)

    for w in range(4):
        def finish(p, w=w):
            across(w, p, a, b, own(w, p)).wait_send()
            both_ways(w, p, a, b, own(w, p), sent)
            pltpu.make_async_copy(
                own(w, p), slot(w, a, b, p), local_sem.at[w * parts + p]).wait()

        each(none, full, w, finish)
        each(split, full, w, lambda p, w=w: both_ways(w, p, a, 1 - b, None, sent))
    lax.fori_loop(1, lines, hop_sent, 0)


def gather_weights(wq, wk, wv, wo):
    count = lax.axis_size("dp")
    lines = count // 2
    parts = max(1, 16 // lines)
    crossed = (1, 1, 1, 0) if parts > 1 else (0, 0, 0, 0)
    units = 4 * parts
    rows, width = wq.shape
    tall = jax.ShapeDtypeStruct((rows * count, width), wq.dtype)
    wide = jax.ShapeDtypeStruct((wo.shape[0], wo.shape[1] * count), wo.dtype)
    dma = pltpu.SemaphoreType.DMA
    return pl.pallas_call(
        functools.partial(gather_kernel, lines, parts, crossed),
        out_shape=(tall, tall, tall, wide),
        in_specs=[pl.BlockSpec(memory_space=pl.ANY)] * 4,
        out_specs=[pl.BlockSpec(memory_space=pl.ANY)] * 4,
        scratch_shapes=[
            dma((2, units, lines)), dma((2, units, lines)), dma((2, units, lines)),
            dma((units, lines)), dma((units, lines)), dma((units,)),
        ],
        compiler_params=pltpu.CompilerParams(collective_id=0, has_side_effects=True),
    )(wq, wk, wv, wo)


def segment_ids(lengths, count):
    ends = jnp.cumsum(lengths, axis=-1)
    position = jnp.arange(count, dtype=jnp.int32)
    above = (position[None, :, None] >= ends[:, None, :-1]).astype(jnp.int32)
    return jnp.sum(above, axis=-1)


def rms_norm(inputs, norm_gain):
    floats = inputs.astype(jnp.float32)
    spread = jnp.sqrt(jnp.mean(floats * floats, axis=-1, keepdims=True) + epsilon)
    normal = floats / spread
    return (normal * norm_gain, normal, spread)


def norm_back(grad_out, normal, spread, norm_gain):
    scaled = grad_out * norm_gain
    return (scaled - normal * jnp.mean(scaled * normal, axis=-1, keepdims=True)) / spread


def dot(left, right):
    return jnp.dot(left, right, preferred_element_type=jnp.float32)


def dot_t(left, right):
    return lax.dot_general(left, right, (((1,), (1,)), ((), ())), preferred_element_type=jnp.float32)


def heads_of(rows, micro):
    return rows.reshape(micro, rows.shape[0] // micro, -1, HD)


def heads_einsum(spec, left, right):
    return jnp.einsum(spec, left, right, preferred_element_type=jnp.float32)


def softmax_scores(query, key, same_doc):
    scores = heads_einsum("mqhd,mkhd->mhqk", query, key) * HD ** (-0.5)
    scores = jnp.where(same_doc[:, None], scores, -1e30)
    exponent = jnp.exp(scores - jnp.max(scores, axis=-1, keepdims=True))
    return exponent / jnp.sum(exponent, axis=-1, keepdims=True)


def partner(array, axis):
    return lax.ppermute(array, axis, [(0, 1), (1, 0)])


def sum_of_all(array):
    array = array + partner(array, "mp")
    count = lax.axis_size("dp")
    step = 1
    while step < count:
        array = array + lax.ppermute(array, "dp", [(i, i ^ step) for i in range(count)])
        step *= 2
    return array


def shards(
    enc_input, dec_input, enc_lengths, dec_lengths, w_query, w_key, w_value, w_output,
    layer_gains, final_gain, cotangent,
):
    is_encoder = lax.axis_index("section") == 0
    core = lax.axis_index("mp")
    micro, piece, width = enc_input.shape[1:]
    count = piece * lax.axis_size("mp")
    rows = micro * count
    gain = layer_gains[0]

    def all_rows(pieces):
        return lax.all_gather(pieces, "mp", axis=1, tiled=True).reshape(rows, width)

    def add_pieces(partial_rows):
        halves = partial_rows.astype(jnp.bfloat16).reshape(micro, 2, piece, width)
        mine = lax.dynamic_index_in_dim(halves, core, 1, keepdims=False)
        other = lax.dynamic_index_in_dim(halves, 1 - core, 1, keepdims=False)
        return mine.astype(jnp.float32) + partner(other, "mp").astype(jnp.float32)

    enc_seg = segment_ids(enc_lengths[0], count)
    dec_seg = segment_ids(dec_lengths[0], count)
    query_seg = jnp.where(is_encoder, enc_seg, dec_seg)
    same_doc = query_seg[:, :, None] == enc_seg[:, None, :]
    entry = jnp.where(is_encoder, enc_input[0], dec_input[0])
    inputs = all_rows(entry)
    grad_last = all_rows(cotangent[0])
    full_q, full_k, full_v, full_o = gather_weights(
        w_query[0], w_key[0], w_value[0], w_output[0]
    )
    hidden_f, normal, spread = rms_norm(inputs, gain)
    hidden = hidden_f.astype(jnp.bfloat16)
    query = heads_of(dot(hidden, full_q).astype(jnp.bfloat16), micro)

    def forward(source):
        key = heads_of(dot(source, full_k).astype(jnp.bfloat16), micro)
        value = heads_of(dot(source, full_v).astype(jnp.bfloat16), micro)
        attention = softmax_scores(query, key, same_doc)
        mixed = heads_einsum("mhqk,mkhd->mqhd", attention.astype(jnp.bfloat16), value)
        part = dot(mixed.astype(jnp.bfloat16).reshape(rows, -1), full_o)
        result = (entry.astype(jnp.float32) + add_pieces(part)).astype(jnp.bfloat16)
        return result, key, value, attention

    enc_out = forward(hidden)[0]
    from_enc = lax.ppermute(enc_out, "section", [(0, 1)])
    encoded = jnp.where(is_encoder, enc_out, from_enc)
    normed, enc_normal, enc_spread = rms_norm(encoded, final_gain)
    source = jnp.where(is_encoder, hidden, all_rows(normed.astype(jnp.bfloat16)))
    layer_out, key, value, attention = forward(source)
    attention_b = attention.astype(jnp.bfloat16)

    def score_grads(grad_rows):
        grad_mixed = heads_of(dot_t(grad_rows, full_o).astype(jnp.bfloat16), micro)
        grad_value = heads_einsum("mhqk,mqhd->mkhd", attention_b, grad_mixed)
        grad_att = heads_einsum("mqhd,mkhd->mhqk", grad_mixed, value)
        shared = jnp.sum(attention * grad_att, axis=-1, keepdims=True)
        grad_scores = (attention * (grad_att - shared) * HD ** (-0.5)).astype(jnp.bfloat16)
        grad_key = heads_einsum("mhqk,mqhd->mkhd", grad_scores, query)
        grad_source = dot_t(grad_key.astype(jnp.bfloat16).reshape(rows, -1), full_k)
        grad_source = grad_source + dot_t(
            grad_value.astype(jnp.bfloat16).reshape(rows, -1), full_v
        )
        return grad_scores, grad_source

    cross = add_pieces(score_grads(grad_last)[1])
    cross_sent = lax.ppermute(cross.astype(jnp.bfloat16), "section", [(1, 0)])
    cross = jnp.where(is_encoder, cross_sent, cross.astype(jnp.bfloat16)).astype(jnp.float32)
    enc_grads = norm_back(cross, enc_normal, enc_spread, final_gain).astype(jnp.bfloat16)
    final_part = jnp.sum(cross * enc_normal, axis=(0, 1))

    grad_piece = jnp.where(is_encoder, enc_grads, cotangent[0])
    grad_rows = all_rows(grad_piece)
    grad_scores, grad_source = score_grads(grad_rows)
    grad_query = heads_einsum("mhqk,mkhd->mqhd", grad_scores, key)
    grad_hidden = dot_t(grad_query.astype(jnp.bfloat16).reshape(rows, -1), full_q)
    grad_hidden = grad_hidden + jnp.where(is_encoder, grad_source, 0.0)
    grad_part = norm_back(grad_hidden, normal, spread, gain)
    gain_part = jnp.sum(grad_hidden * normal, axis=0)
    totals = sum_of_all(jnp.stack([gain_part, final_part]))
    input_grad = (grad_piece.astype(jnp.float32) + add_pieces(grad_part)).astype(jnp.bfloat16)
    return (layer_out[None, None], input_grad[None, None], totals[:1], totals[1])


def solution(mesh):
    return jax.shard_map(
        shards,
        mesh=mesh,
        in_specs=(
            P("dp", None, "mp", None),
            P("dp", None, "mp", None),
            P("dp", None, None),
            P("dp", None, None),
            P("section", "dp", "mp"),
            P("section", "dp", "mp"),
            P("section", "dp", "mp"),
            P("section", "mp", "dp"),
            P("section", None),
            P(),
            P("dp", None, "mp", None),
        ),
        out_specs=(
            P("section", "dp", None, "mp", None),
            P("section", "dp", None, "mp", None),
            P("section", None),
            P(),
        ),
        check_vma=False,
    )
```

```python
import functools

import jax
import jax.numpy as jnp
from jax import lax
from jax.experimental import pallas as pl
from jax.experimental.pallas import tpu as pltpu
from jax.sharding import PartitionSpec as P

HD = 256
MESH = pl.DeviceIdType.MESH

epsilon = 1e-06


def gather_kernel(
    lines, parts, crossed, wq, wk, wv, wo, oq, ok, ov, oo,
    send_right, send_left, recv_z, send_y, recv_y, local_sem,
):
    me = lax.axis_index("dp")
    a = me // 2
    b = me % 2
    ins = (wq, wk, wv, wo)
    outs = (oq, ok, ov, oo)

    def own(w, p):
        size = ins[w].shape[0] // parts
        return ins[w].at[pl.ds(pl.multiple_of(p * size, size), size), :]

    def slot(w, line, side, p):
        size = ins[w].shape[0] // parts
        block = line * 2 + side
        if w < 3:
            start = block * ins[w].shape[0] + p * size
            return outs[w].at[pl.ds(pl.multiple_of(start, size), size), :]
        cols = ins[w].shape[1]
        return outs[w].at[
            pl.ds(pl.multiple_of(p * size, size), size),
            pl.ds(pl.multiple_of(block * cols, cols), cols),
        ]

    def along(w, p, line, side, right, src=None):
        dst = slot(w, line, side, p)
        sem = (send_right if right else send_left).at[side, w * parts + p, line]
        target = (a + 1) if right else (a - 1)
        return pltpu.make_async_remote_copy(
            src_ref=dst if src is None else src, dst_ref=dst, send_sem=sem,
            recv_sem=recv_z.at[side, w * parts + p, line],
            device_id={"dp": target * 2 + b}, device_id_type=MESH,
        )

    def across(w, p, line, side, src=None):
        dst = slot(w, line, side, p)
        return pltpu.make_async_remote_copy(
            src_ref=dst if src is None else src, dst_ref=dst,
            send_sem=send_y.at[w * parts + p, line],
            recv_sem=recv_y.at[w * parts + p, line],
            device_id={"dp": a * 2 + 1 - b}, device_id_type=MESH,
        )

    def each(first, last, w, body):
        if last[w] > first[w]:
            lax.fori_loop(first[w], last[w], lambda p, c: (body(p), c)[1], 0)

    none = [0] * 4
    split = [parts - crossed[w] for w in range(4)]
    full = [parts] * 4
    has_right = a + 1 < lines
    has_left = a > 0

    barrier = pltpu.get_barrier_semaphore()
    pl.semaphore_signal(barrier, inc=1, device_id={"dp": a * 2 + 1 - b}, device_id_type=MESH)

    @pl.when(has_right)
    def _():
        pl.semaphore_signal(barrier, inc=1, device_id={"dp": me + 2}, device_id_type=MESH)

    @pl.when(has_left)
    def _():
        pl.semaphore_signal(barrier, inc=1, device_id={"dp": me - 2}, device_id_type=MESH)

    peers = 1 + has_right.astype(jnp.int32) + has_left.astype(jnp.int32)
    pl.semaphore_wait(barrier, peers)

    def both_ways(w, p, line, side, src, op):
        @pl.when(has_right)
        def _():
            op(along(w, p, line, side, True, src))

        @pl.when(has_left)
        def _():
            op(along(w, p, line, side, False, src))

    def start(copy):
        copy.start()

    def sent(copy):
        copy.wait_send()

    def begin_across(w, p):
        across(w, p, a, b, own(w, p)).start()

    def begin_along(w, p):
        both_ways(w, p, a, b, own(w, p), start)

    def begin(w, p):
        begin_along(w, p)
        begin_across(w, p)

    for w in range(4):
        each(split, full, w, functools.partial(begin_across, w))
    for w in range(4):
        each(none, split, w, functools.partial(begin, w))
    for w in range(4):
        each(split, full, w, functools.partial(begin_along, w))
    for w in range(4):
        each(none, full, w, lambda p, w=w: pltpu.make_async_copy(
            own(w, p), slot(w, a, b, p), local_sem.at[w * parts + p]).start())

    def turn(w, p):
        across(w, p, a, 1 - b).wait_recv()
        both_ways(w, p, a, 1 - b, None, start)

    for w in range(4):
        each(split, full, w, functools.partial(turn, w))

    def relay(w, p, dist, side, cross, op):
        @pl.when(a - dist >= 0)
        def _():
            line = a - dist
            if op is start:
                along(w, p, line, side, True).wait_recv()

            @pl.when(has_right)
            def _():
                op(along(w, p, line, side, True))

            if cross:
                op(across(w, p, line, side))

        @pl.when(a + dist < lines)
        def _():
            line = a + dist
            if op is start:
                along(w, p, line, side, False).wait_recv()

            @pl.when(has_left)
            def _():
                op(along(w, p, line, side, False))

            if cross:
                op(across(w, p, line, side))

    def hop(dist, op):
        for w in range(4):
            each(none, split, w, lambda p, w=w: relay(w, p, dist, b, True, op))
        for w in range(4):
            def crossed_part(p, w=w):
                relay(w, p, dist, b, False, op)
                relay(w, p, dist, 1 - b, False, op)

            each(split, full, w, crossed_part)

    def hop_start(dist, c):
        hop(dist, start)
        return c

    def hop_sent(dist, c):
        hop(dist, sent)
        return c

    lax.fori_loop(1, lines, hop_start, 0)
    for w in range(4):
        def arrived(p, w=w):
            def one(line, c):
                across(w, p, line, 1 - b).wait_recv()
                return c

            lax.fori_loop(0, lines, one, 0)

        each(none, split, w, arrived)

    for w in range(4):
        def finish(p, w=w):
            across(w, p, a, b, own(w, p)).wait_send()
            both_ways(w, p, a, b, own(w, p), sent)
            pltpu.make_async_copy(
                own(w, p), slot(w, a, b, p), local_sem.at[w * parts + p]).wait()

        each(none, full, w, finish)
        each(split, full, w, lambda p, w=w: both_ways(w, p, a, 1 - b, None, sent))
    lax.fori_loop(1, lines, hop_sent, 0)


def gather_weights(wq, wk, wv, wo):
    count = lax.axis_size("dp")
    lines = count // 2
    parts = max(1, 16 // lines)
    crossed = (1, 1, 1, 0) if parts > 1 else (0, 0, 0, 0)
    units = 4 * parts
    rows, width = wq.shape
    tall = jax.ShapeDtypeStruct((rows * count, width), wq.dtype)
    wide = jax.ShapeDtypeStruct((wo.shape[0], wo.shape[1] * count), wo.dtype)
    dma = pltpu.SemaphoreType.DMA
    return pl.pallas_call(
        functools.partial(gather_kernel, lines, parts, crossed),
        out_shape=(tall, tall, tall, wide),
        in_specs=[pl.BlockSpec(memory_space=pl.ANY)] * 4,
        out_specs=[pl.BlockSpec(memory_space=pl.ANY)] * 4,
        scratch_shapes=[
            dma((2, units, lines)), dma((2, units, lines)), dma((2, units, lines)),
            dma((units, lines)), dma((units, lines)), dma((units,)),
        ],
        compiler_params=pltpu.CompilerParams(collective_id=0, has_side_effects=True),
    )(wq, wk, wv, wo)


def segment_ids(lengths, count):
    ends = jnp.cumsum(lengths, axis=-1)
    position = jnp.arange(count, dtype=jnp.int32)
    above = (position[None, :, None] >= ends[:, None, :-1]).astype(jnp.int32)
    return jnp.sum(above, axis=-1)


def rms_norm(inputs, norm_gain):
    floats = inputs.astype(jnp.float32)
    spread = jnp.sqrt(jnp.mean(floats * floats, axis=-1, keepdims=True) + epsilon)
    normal = floats / spread
    return (normal * norm_gain, normal, spread)


def norm_back(grad_out, normal, spread, norm_gain):
    scaled = grad_out * norm_gain
    return (scaled - normal * jnp.mean(scaled * normal, axis=-1, keepdims=True)) / spread


def dot(left, right):
    return jnp.dot(left, right, preferred_element_type=jnp.float32)


def dot_t(left, right):
    return lax.dot_general(left, right, (((1,), (1,)), ((), ())), preferred_element_type=jnp.float32)


def heads_of(rows, micro):
    return rows.reshape(micro, rows.shape[0] // micro, -1, HD)


def heads_einsum(spec, left, right):
    return jnp.einsum(spec, left, right, preferred_element_type=jnp.float32)


def softmax_scores(query, key, same_doc):
    scores = heads_einsum("mqhd,mkhd->mhqk", query, key) * HD ** (-0.5)
    scores = jnp.where(same_doc[:, None], scores, -1e30)
    exponent = jnp.exp(scores - jnp.max(scores, axis=-1, keepdims=True))
    return exponent / jnp.sum(exponent, axis=-1, keepdims=True)


def partner(array, axis):
    return lax.ppermute(array, axis, [(0, 1), (1, 0)])


def after(array, other):
    return array + (0.0 * other[0, 0].astype(jnp.float32)).astype(array.dtype)


def sum_of_all(array):
    array = array + partner(array, "mp")
    count = lax.axis_size("dp")
    step = 1
    while step < count:
        array = array + lax.ppermute(array, "dp", [(i, i ^ step) for i in range(count)])
        step *= 2
    return array


def shards(
    enc_input, dec_input, enc_lengths, dec_lengths, w_query, w_key, w_value, w_output,
    layer_gains, final_gain, cotangent,
):
    is_encoder = lax.axis_index("section") == 0
    core = lax.axis_index("mp")
    micro, piece, width = enc_input.shape[1:]
    count = piece * lax.axis_size("mp")
    rows = micro * count
    gain = layer_gains[0]

    def all_rows(pieces):
        return lax.all_gather(pieces, "mp", axis=1, tiled=True).reshape(rows, width)

    def add_pieces(partial_rows):
        halves = partial_rows.astype(jnp.bfloat16).reshape(micro, 2, piece, width)
        mine = lax.dynamic_index_in_dim(halves, core, 1, keepdims=False)
        other = lax.dynamic_index_in_dim(halves, 1 - core, 1, keepdims=False)
        return mine.astype(jnp.float32) + partner(other, "mp").astype(jnp.float32)

    enc_seg = segment_ids(enc_lengths[0], count)
    dec_seg = segment_ids(dec_lengths[0], count)
    query_seg = jnp.where(is_encoder, enc_seg, dec_seg)
    same_doc = query_seg[:, :, None] == enc_seg[:, None, :]
    entry = jnp.where(is_encoder, enc_input[0], dec_input[0])
    inputs = all_rows(entry)
    grad_last = all_rows(cotangent[0])
    full_q, full_k, full_v, full_o = gather_weights(
        w_query[0], w_key[0], w_value[0], w_output[0]
    )
    hidden_f, normal, spread = rms_norm(inputs, gain)
    hidden = hidden_f.astype(jnp.bfloat16)
    query = heads_of(dot(hidden, full_q).astype(jnp.bfloat16), micro)

    def forward(source):
        key = heads_of(dot(source, full_k).astype(jnp.bfloat16), micro)
        value = heads_of(dot(source, full_v).astype(jnp.bfloat16), micro)
        attention = softmax_scores(query, key, same_doc)
        mixed = heads_einsum("mhqk,mkhd->mqhd", attention.astype(jnp.bfloat16), value)
        part = dot(mixed.astype(jnp.bfloat16).reshape(rows, -1), full_o)
        result = (entry.astype(jnp.float32) + add_pieces(part)).astype(jnp.bfloat16)
        return result, key, value, attention, part

    enc_out = forward(hidden)[0]
    mixed_last = dot_t(grad_last, full_o).astype(jnp.bfloat16)
    from_enc = after(lax.ppermute(enc_out, "section", [(0, 1)]), mixed_last)
    encoded = jnp.where(is_encoder, enc_out, from_enc)
    normed, enc_normal, enc_spread = rms_norm(encoded, final_gain)
    source = jnp.where(is_encoder, hidden, all_rows(normed.astype(jnp.bfloat16)))
    layer_out, key, value, attention, last_part = forward(source)
    attention_b = attention.astype(jnp.bfloat16)

    def score_grads(mixed_rows):
        grad_mixed = heads_of(mixed_rows, micro)
        grad_value = heads_einsum("mhqk,mqhd->mkhd", attention_b, grad_mixed)
        grad_att = heads_einsum("mqhd,mkhd->mhqk", grad_mixed, value)
        shared = jnp.sum(attention * grad_att, axis=-1, keepdims=True)
        grad_scores = (attention * (grad_att - shared) * HD ** (-0.5)).astype(jnp.bfloat16)
        grad_key = heads_einsum("mhqk,mqhd->mkhd", grad_scores, query)
        grad_source = dot_t(grad_key.astype(jnp.bfloat16).reshape(rows, -1), full_k)
        grad_source = grad_source + dot_t(
            grad_value.astype(jnp.bfloat16).reshape(rows, -1), full_v
        )
        return grad_scores, grad_source

    cross = add_pieces(score_grads(mixed_last)[1])
    cross_sent = lax.ppermute(cross.astype(jnp.bfloat16), "section", [(1, 0)])
    cross_sent = after(cross_sent, last_part)
    cross = jnp.where(is_encoder, cross_sent, cross.astype(jnp.bfloat16)).astype(jnp.float32)
    enc_grads = norm_back(cross, enc_normal, enc_spread, final_gain).astype(jnp.bfloat16)
    final_part = jnp.sum(cross * enc_normal, axis=(0, 1))

    grad_piece = jnp.where(is_encoder, enc_grads, cotangent[0])
    grad_rows = all_rows(grad_piece)
    grad_scores, grad_source = score_grads(dot_t(grad_rows, full_o).astype(jnp.bfloat16))
    grad_query = heads_einsum("mhqk,mkhd->mqhd", grad_scores, key)
    grad_hidden = dot_t(grad_query.astype(jnp.bfloat16).reshape(rows, -1), full_q)
    grad_hidden = grad_hidden + jnp.where(is_encoder, grad_source, 0.0)
    grad_part = norm_back(grad_hidden, normal, spread, gain)
    gain_part = jnp.sum(grad_hidden * normal, axis=0)
    totals = sum_of_all(jnp.stack([gain_part, final_part]))
    input_grad = (grad_piece.astype(jnp.float32) + add_pieces(grad_part)).astype(jnp.bfloat16)
    return (layer_out[None, None], input_grad[None, None], totals[:1], totals[1])


def solution(mesh):
    return jax.shard_map(
        shards,
        mesh=mesh,
        in_specs=(
            P("dp", None, "mp", None),
            P("dp", None, "mp", None),
            P("dp", None, None),
            P("dp", None, None),
            P("section", "dp", "mp"),
            P("section", "dp", "mp"),
            P("section", "dp", "mp"),
            P("section", "mp", "dp"),
            P("section", None),
            P(),
            P("dp", None, "mp", None),
        ),
        out_specs=(
            P("section", "dp", None, "mp", None),
            P("section", "dp", None, "mp", None),
            P("section", None),
            P(),
        ),
        check_vma=False,
    )
```
